32 devices in a mesh: src: 4 (over x, core), tgt: 8 (over z, y).
Axes of the slice: x: 2, y: 2, z: 4, core: 2. Of those that a mesh axis runs over, the one named last changes fastest.
Arguments:
- source_feat: bfloat16 [4096, 256], P(('src', 'tgt')), may hold values from -40 to 40
- target_feat: bfloat16 [14400, 256], P('tgt', 'src'), may hold values from -4 to 4
- proj: bfloat16 [256, 256], replicated, may hold values from -0.375 to 0.375
Outputs:
- flow: float32 [2, 4096], P(None, ('src', 'tgt'))
- matched: bfloat16 [4096, 256], P(('src', 'tgt'))
The draws below stay inside these ranges and needn't reach their ends.
All inputs are finite; a program needn't handle non-finite values.
Results may differ from the reference program's by a relative error of at most 0.0075.
Values may be sent and summed in bfloat16 or wider, within the bound.
No kernel may reach another device: no remote copies, remote signals or barrier semaphores. Data moves between devices by JAX's collectives and lax.ppermute only.
A program may use at most 256 MiB of HBM per device.

```python
import math
import jax
import jax.numpy as jnp
from jax import lax

C = 256
W_GRID = 320
SOURCES = 4096
TARGETS = 14400


def target_table(key):
    base = jax.random.fold_in(key, 11)
    table = jnp.clip(jax.random.normal(base, (TARGETS, C), jnp.float32), -4.0, 4.0)
    return table


def draw_target_feat(key, part):
    return target_table(key).astype(jnp.bfloat16)


def draw_source_feat(key, part):
    scale_key = jax.random.fold_in(key, 23)
    value_key = jax.random.fold_in(key, 37)
    row_scale = jnp.exp(jax.random.uniform(scale_key, (SOURCES,), jnp.float32, math.log(0.3), math.log(2.0)))
    values = jnp.clip(jax.random.normal(value_key, (SOURCES, C), jnp.float32), -6.0, 6.0) * row_scale[:, None]
    return values.astype(jnp.bfloat16)


def scatter_about(own_key, dims, deviation, most, kind=jnp.bfloat16):
    array = deviation * jax.random.normal(own_key, dims, jnp.float32)
    return jnp.clip(array, min=-most, max=most).astype(kind)


def setup_inputs(seed: int = 0) -> dict:
    key_list = jax.random.split(jax.random.key(seed), 4)
    return {
        "source_feat": draw_source_feat(jax.random.fold_in(key_list[3], 71), 0),
        "target_feat": draw_target_feat(jax.random.fold_in(key_list[3], 71), 0),
        "proj": scatter_about(key_list[2], (C, C), C ** -0.5, 0.375),
    }


def reference(source_feat, target_feat, proj):
    queries = jnp.dot(source_feat, proj, preferred_element_type=jnp.float32).astype(jnp.bfloat16)
    keys = jnp.dot(target_feat, proj, preferred_element_type=jnp.float32).astype(jnp.bfloat16)
    width = queries.shape[1]
    count = keys.shape[0]
    pos = jnp.arange(count, dtype=jnp.int32)
    grid_x = (pos % W_GRID).astype(jnp.float32) / W_GRID
    grid_y = (pos // W_GRID).astype(jnp.float32) / W_GRID
    rows = queries.shape[0]
    block = min(256, rows)
    blocks = queries.reshape(rows // block, block, width)

    def one_block(qblock):
        scores = jnp.einsum("qc,kc->qk", qblock, keys, preferred_element_type=jnp.float32) * (width ** -0.5)
        top = jnp.max(scores, axis=1)
        weights = jnp.exp(scores - top[:, None])
        total = jnp.sum(weights, axis=1)
        coord_x = jnp.sum(weights * grid_x[None, :], axis=1)
        coord_y = jnp.sum(weights * grid_y[None, :], axis=1)
        feat_sum = jnp.dot(weights.astype(jnp.bfloat16), keys, preferred_element_type=jnp.float32)
        return total, coord_x, coord_y, feat_sum

    total, coord_x, coord_y, feat_sum = lax.map(one_block, blocks)
    total = total.reshape(rows)
    coord_x = coord_x.reshape(rows)
    coord_y = coord_y.reshape(rows)
    feat_sum = feat_sum.reshape(rows, width)
    own = jnp.arange(rows, dtype=jnp.int32)
    own_x = (own % W_GRID).astype(jnp.float32) / W_GRID
    own_y = (own // W_GRID).astype(jnp.float32) / W_GRID
    flow = jnp.stack([coord_x / total - own_x, coord_y / total - own_y], axis=0)
    matched = (feat_sum / total[:, None]).astype(jnp.bfloat16)
    return flow, matched
```

```python
import functools
import math

import jax
import jax.numpy as jnp
from jax import lax
from jax.experimental import pallas as pl
from jax.experimental.pallas import tpu as pltpu
from jax.sharding import PartitionSpec as P

W_GRID = 320
STAT_ROWS = 16
F32, BF16 = jnp.float32, jnp.bfloat16


def grid_coords(pos):
    return (
        (pos % W_GRID).astype(F32) / W_GRID,
        (pos // W_GRID).astype(F32) / W_GRID,
    )


def coord_rows(start, count):
    pos = start + lax.broadcasted_iota(jnp.int32, (STAT_ROWS, count), 1)
    row = lax.broadcasted_iota(jnp.int32, (STAT_ROWS, count), 0)
    gx, gy = pos % W_GRID, pos // W_GRID
    rows = jnp.where(row == 0, 1, 0)
    for index, value in enumerate((gx // 16, gx % 16, gy // 16, gy % 16)):
        rows = jnp.where(row == index + 1, value, rows)
    return rows.astype(BF16)


def split3(value):
    high = value.astype(BF16)
    rest = value - high.astype(F32)
    mid = rest.astype(BF16)
    low = (rest - mid.astype(F32)).astype(BF16)
    return [high.astype(F32), mid.astype(F32), low.astype(F32)]


def attend(pieces, projt, rows, queries, scale, kext):
    width = projt.shape[0]
    strip = jnp.concatenate([p[...] for p in pieces], axis=0)
    kext[0:width, :] = jnp.dot(projt[...], strip, preferred_element_type=F32).astype(BF16)
    kext[width:, :] = rows[...]
    raw = jnp.dot(queries, kext[0:width, :], preferred_element_type=F32)
    top = jnp.max(raw, axis=1, keepdims=True)
    weights = jnp.exp2((raw - top) * scale).astype(BF16)
    sums = lax.dot_general(
        kext[...], weights, (((1,), (1,)), ((), ())), preferred_element_type=F32
    )
    return top, sums


def as_row(column):
    return jnp.transpose(jnp.broadcast_to(column, (column.shape[0], 128)))[0:1, :]


def first_kernel(n_src, scale, *refs):
    pieces, (projt, proj, rows), refs = refs[:n_src], refs[n_src : n_src + 3], refs[n_src + 3 :]
    *sources, top_ref, sums_ref, query_ref, kext = refs
    source = jnp.concatenate([s[...] for s in sources], axis=0)
    queries = jnp.dot(source, proj[...], preferred_element_type=F32).astype(BF16)
    query_ref[...] = queries
    top, sums = attend(pieces, projt, rows, queries, scale, kext)
    top_ref[...] = as_row(top)
    sums_ref[...] = sums


def second_kernel(n_src, scale, *refs):
    pieces = refs[:n_src]
    projt, rows, query_ref, top_ref, sums_ref, out_ref, kext = refs[n_src:]
    top2, sums2 = attend(pieces, projt, rows, query_ref[...], scale, kext)
    top1, top2 = top_ref[...], as_row(top2)
    top = jnp.maximum(top1, top2)
    sums = sums_ref[...] * jnp.exp2((top1 - top) * scale) + sums2 * jnp.exp2((top2 - top) * scale)
    width = sums.shape[0] - STAT_ROWS
    stats = sums[width:]
    coord_x = stats[1:2] * 16.0 + stats[2:3]
    coord_y = stats[3:4] * 16.0 + stats[4:5]
    parts = split3(top) + split3(stats[0:1]) + split3(coord_x) + split3(coord_y)
    parts.append(jnp.zeros((STAT_ROWS - len(parts), top.shape[1]), F32))
    tail = jnp.concatenate(parts, axis=0).astype(BF16)
    blocks, _, lanes = out_ref.shape
    for index in range(blocks):
        cols = slice(index * lanes, (index + 1) * lanes)
        out_ref[index, 0:width, :] = sums[0:width, cols].astype(BF16)
        out_ref[index, width:, :] = tail[:, cols]


def merge_kernel(scale, *refs):
    *parts, own_ref, flow_ref, matched_ref = refs
    width = matched_ref.shape[1]
    stats = [p[width:, :].astype(F32) for p in parts]
    join = lambda s, k: s[3 * k : 3 * k + 1] + s[3 * k + 1 : 3 * k + 2] + s[3 * k + 2 : 3 * k + 3]
    tops = [join(s, 0) for s in stats]
    top = functools.reduce(jnp.maximum, tops)
    factors = [jnp.exp2((t - top) * scale) for t in tops]
    total, coord_x, coord_y = (
        sum(f * join(s, k) for f, s in zip(factors, stats)) for k in (1, 2, 3)
    )
    feat = sum(f * p[0:width, :].astype(F32) for f, p in zip(factors, parts))
    flow_ref[0:1, :] = coord_x / (total * W_GRID) - own_ref[0:1, :]
    flow_ref[1:2, :] = coord_y / (total * W_GRID) - own_ref[1:2, :]
    matched_ref[...] = jnp.transpose(feat / total).astype(matched_ref.dtype)


def call(kernel, outs, scratch, flops, args):
    size = lambda a: math.prod(a.shape) * a.dtype.itemsize
    return pl.pallas_call(
        kernel,
        out_shape=outs,
        scratch_shapes=scratch,
        compiler_params=pltpu.CompilerParams(vmem_limit_bytes=40 * 2**20),
        cost_estimate=pl.CostEstimate(
            flops=flops,
            bytes_accessed=sum(map(size, args)) + sum(map(size, jax.tree.leaves(outs))),
            transcendentals=0,
        ),
    )(*args)


def per_device(source_feat, target_feat, proj):
    width = proj.shape[1]
    own_rows = source_feat.shape[0]
    count, depth = target_feat.shape
    n_src, n_tgt = lax.axis_size("src"), lax.axis_size("tgt")
    src, tgt = lax.axis_index("src"), lax.axis_index("tgt")
    scale = math.log2(math.e) * width ** (-0.5)
    axes = ("src", "tgt")

    def swap(x, s=0, t=0):
        pairs = [
            (a * n_tgt + b, (a ^ s) * n_tgt + (b ^ t)) for a in range(n_src) for b in range(n_tgt)
        ]
        return lax.ppermute(x, axes, pairs)

    strip = target_feat.T
    far = [swap(strip, s=2), swap(strip, t=1), swap(strip, s=2, t=1)]
    near = swap(strip, s=1)
    sources = [source_feat] + [swap(source_feat, t=2 * k) for k in range(1, n_tgt // 2)]
    near_far = [swap(x, s=1) for x in far]
    first = [strip, near, far[0], near_far[0]]
    second = [far[1], near_far[1], far[2], near_far[2]]

    order = src ^ jnp.arange(n_src, dtype=jnp.int32)
    projt = jnp.take(proj.reshape(n_src, depth, width), order, axis=0).reshape(width, width).T
    rows = [coord_rows((tgt ^ k) * count, count) for k in (0, 1)]

    n_q = own_rows * len(sources)
    ext = width + STAT_ROWS
    shape = jax.ShapeDtypeStruct
    flops = 2 * count * width * (width + 2 * n_q)
    kext = [pltpu.VMEM((ext, count), BF16)]
    top, sums, queries = call(
        functools.partial(first_kernel, n_src, scale),
        (shape((1, n_q), F32), shape((ext, n_q), F32), shape((n_q, width), BF16)),
        kext,
        flops,
        (*first, projt, proj, rows[0], *sources),
    )
    message = call(
        functools.partial(second_kernel, n_src, scale),
        shape((len(sources), ext, own_rows), BF16),
        kext,
        flops,
        (*second, projt, rows[1], queries, top, sums),
    )
    parts = [message[0]] + [swap(message[k], t=2 * k) for k in range(1, len(sources))]
    own_pos = (src * n_tgt + tgt) * own_rows + jnp.arange(own_rows, dtype=jnp.int32)
    own = jnp.stack(grid_coords(own_pos), axis=0)
    return call(
        functools.partial(merge_kernel, scale),
        (shape((2, own_rows), F32), shape((own_rows, width), BF16)),
        [],
        4 * ext * own_rows * len(parts),
        (*parts, own),
    )


def solution(mesh):
    in_specs = (P(("src", "tgt"), None), P("tgt", "src"), P())
    out_specs = (P(None, ("src", "tgt")), P(("src", "tgt"), None))
    return jax.shard_map(
        per_device, mesh=mesh, in_specs=in_specs, out_specs=out_specs, check_vma=False
    )
```

```python
import functools
import math

import jax
import jax.numpy as jnp
from jax import lax
from jax.experimental import pallas as pl
from jax.experimental.pallas import tpu as pltpu
from jax.sharding import PartitionSpec as P

W_GRID = 320
STAT_ROWS = 16
F32, BF16 = jnp.float32, jnp.bfloat16


def grid_coords(pos):
    return (
        (pos % W_GRID).astype(F32) / W_GRID,
        (pos // W_GRID).astype(F32) / W_GRID,
    )


def coord_rows(start, count):
    pos = start + lax.broadcasted_iota(jnp.int32, (STAT_ROWS, count), 1)
    row = lax.broadcasted_iota(jnp.int32, (STAT_ROWS, count), 0)
    gx, gy = pos % W_GRID, pos // W_GRID
    rows = jnp.where(row == 0, 1, 0)
    for index, value in enumerate((gx // 16, gx % 16, gy // 16, gy % 16)):
        rows = jnp.where(row == index + 1, value, rows)
    return rows.astype(BF16)


def split3(value):
    high = value.astype(BF16)
    rest = value - high.astype(F32)
    mid = rest.astype(BF16)
    low = (rest - mid.astype(F32)).astype(BF16)
    return [high.astype(F32), mid.astype(F32), low.astype(F32)]


def project(pieces, projt, rows, strip, kext):
    depth, width = pieces[0].shape[0], projt.shape[0]
    src = lax.axis_index("src")
    for step, piece in enumerate(pieces):
        strip[pl.ds(pl.multiple_of((src ^ step) * depth, depth), depth), :] = piece
    kext[0:width, :] = jnp.dot(projt[...], strip[...], preferred_element_type=F32).astype(BF16)
    kext[width:, :] = rows[...]


def attend(queries, kext, scale):
    width = queries.shape[1]
    raw = jnp.dot(queries, kext[0:width, :], preferred_element_type=F32)
    top = jnp.max(raw, axis=1, keepdims=True)
    weights = jnp.exp2((raw - top) * scale).astype(BF16)
    sums = lax.dot_general(
        kext[...], weights, (((1,), (1,)), ((), ())), preferred_element_type=F32
    )
    return as_row(top), sums


def as_row(column):
    return jnp.transpose(jnp.broadcast_to(column, (column.shape[0], 128)))[0:1, :]


def pick(even, odd):
    return jnp.where(lax.axis_index("src") % 2 == 0, even[...], odd[...])


def first_kernel(scale, *refs):
    own, near, one, near_one, two, near_two, projt, proj, rows, source, *refs = refs
    top_ref, sums_ref, query_ref, kext, strip = refs
    queries = jnp.dot(source[...], proj[...], preferred_element_type=F32).astype(BF16)
    query_ref[...] = queries
    pieces = [own[...], near[...], pick(one, near_two), pick(two, near_one)]
    project(pieces, projt, rows, strip, kext)
    top_ref[...], sums_ref[...] = attend(queries[0 : top_ref.shape[1]], kext, scale)


def rest_kernel(scale, query_ref, kext, top_ref, sums_ref):
    count = top_ref.shape[1]
    top_ref[...], sums_ref[...] = attend(query_ref[count:, :], kext, scale)


def emit(queries, kext, top1, sums1, scale):
    top2, sums2 = attend(queries, kext, scale)
    top = jnp.maximum(top1, top2)
    sums = sums1 * jnp.exp2((top1 - top) * scale) + sums2 * jnp.exp2((top2 - top) * scale)
    stats = sums[queries.shape[1] :]
    coord_x = stats[1:2] * 16.0 + stats[2:3]
    coord_y = stats[3:4] * 16.0 + stats[4:5]
    parts = split3(top) + split3(stats[0:1]) + split3(coord_x) + split3(coord_y)
    parts.append(jnp.zeros((STAT_ROWS - len(parts), top.shape[1]), F32))
    return jnp.concatenate([sums[0 : queries.shape[1]], *parts], axis=0).astype(BF16)


def second_kernel(scale, *refs):
    one, near_one, two, near_two, cross, near_cross, projt, rows, *refs = refs
    query_ref, top_near, sums_near, top_far, sums_far, out_ref, kext, strip = refs
    pieces = [pick(near_two, one), pick(near_one, two), cross[...], near_cross[...]]
    project(pieces, projt, rows, strip, kext)
    lanes = out_ref.shape[2]
    top1 = jnp.concatenate([top_near[:, lanes:], top_far[...]], axis=1)
    sums1 = jnp.concatenate([sums_near[:, lanes:], sums_far[...]], axis=1)
    out = emit(query_ref[lanes:, :], kext, top1, sums1, scale)
    for index in range(out_ref.shape[0]):
        out_ref[index] = out[:, index * lanes : (index + 1) * lanes]


def last_kernel(scale, query_ref, kext, top_ref, sums_ref, out_ref):
    lanes = out_ref.shape[1]
    out_ref[...] = emit(
        query_ref[0:lanes, :], kext, top_ref[:, 0:lanes], sums_ref[:, 0:lanes], scale
    )


def merge_kernel(scale, *refs):
    *parts, own_ref, flow_ref, matched_ref = refs
    width = matched_ref.shape[1]
    stats = [p[width:, :].astype(F32) for p in parts]
    join = lambda s, k: s[3 * k : 3 * k + 1] + s[3 * k + 1 : 3 * k + 2] + s[3 * k + 2 : 3 * k + 3]
    tops = [join(s, 0) for s in stats]
    top = functools.reduce(jnp.maximum, tops)
    factors = [jnp.exp2((t - top) * scale) for t in tops]
    total, coord_x, coord_y = (
        sum(f * join(s, k) for f, s in zip(factors, stats)) for k in (1, 2, 3)
    )
    feat = sum(f * p[0:width, :].astype(F32) for f, p in zip(factors, parts))
    flow_ref[0:1, :] = coord_x / (total * W_GRID) - own_ref[0:1, :]
    flow_ref[1:2, :] = coord_y / (total * W_GRID) - own_ref[1:2, :]
    matched_ref[...] = jnp.transpose(feat / total).astype(matched_ref.dtype)


def call(kernel, outs, scratch, flops, args):
    size = lambda a: math.prod(a.shape) * a.dtype.itemsize
    return pl.pallas_call(
        kernel,
        out_shape=outs,
        scratch_shapes=scratch,
        compiler_params=pltpu.CompilerParams(vmem_limit_bytes=40 * 2**20),
        cost_estimate=pl.CostEstimate(
            flops=flops,
            bytes_accessed=sum(map(size, args)) + sum(map(size, jax.tree.leaves(outs))),
            transcendentals=0,
        ),
    )(*args)


def after(value, other):
    def kernel(value_ref, other_ref, out_ref):
        out_ref[...] = value_ref[...]

    return pl.pallas_call(
        kernel,
        out_shape=jax.ShapeDtypeStruct(value.shape, value.dtype),
        compiler_params=pltpu.CompilerParams(vmem_limit_bytes=8 * 2**20),
    )(value, other)


def per_device(source_feat, target_feat, proj):
    width = proj.shape[1]
    own_rows = source_feat.shape[0]
    count, depth = target_feat.shape
    n_src, n_tgt = lax.axis_size("src"), lax.axis_size("tgt")
    src, tgt = lax.axis_index("src"), lax.axis_index("tgt")
    scale = math.log2(math.e) * width ** (-0.5)
    axes = ("src", "tgt")

    def permute(x, move):
        pairs = []
        for a in range(n_src):
            for b in range(n_tgt):
                s, t = move(a)
                pairs.append((a * n_tgt + b, (a ^ s) * n_tgt + (b ^ t)))
        return lax.ppermute(x, axes, pairs)

    def swap(x, s=0, t=0):
        return permute(x, lambda a: (s, t))

    turn_one = lambda a: (2, 0) if a % 2 == 0 else (0, 1)
    turn_two = lambda a: (0, 1) if a % 2 == 0 else (2, 0)
    own = target_feat.T
    near = swap(own, s=1)
    one = permute(own, turn_one)
    two = permute(near, turn_one)
    sources, offsets = source_feat, [0]
    for bit in reversed(range(1, n_tgt.bit_length() - 1)):
        sources = jnp.concatenate([sources, swap(sources, t=1 << bit)], axis=0)
        offsets += [offset ^ (1 << bit) for offset in offsets]
    cross = permute(one, turn_two)
    near_one, near_two = swap(one, s=1), swap(two, s=1)

    projt = proj.T
    rows = [coord_rows((tgt ^ k) * count, count) for k in (0, 1)]

    n_q = sources.shape[0]
    blocks = n_q // own_rows
    half = n_q // 2
    ext = width + STAT_ROWS
    shape = jax.ShapeDtypeStruct
    flops = 2 * count * width * (width + 2 * n_q)
    kext = shape((ext, count), BF16)
    strip = [pltpu.VMEM((width, count), BF16)]
    top, sums, queries, keys = call(
        functools.partial(first_kernel, scale),
        (shape((1, half), F32), shape((ext, half), F32), shape((n_q, width), BF16), kext),
        strip,
        flops,
        (own, near, one, near_one, two, near_two, projt, proj, rows[0], sources),
    )
    near_cross = swap(after(cross, top), s=1)
    far_top, far_sums = call(
        functools.partial(rest_kernel, scale),
        (shape((1, half), F32), shape((ext, half), F32)),
        [],
        flops,
        (queries, keys),
    )
    out, keys = call(
        functools.partial(second_kernel, scale),
        (shape((blocks - 1, ext, own_rows), BF16), kext),
        strip,
        flops,
        (one, near_one, two, near_two, cross, near_cross, projt, rows[1], queries)
        + (top, sums, far_top, far_sums),
    )
    kept = call(
        functools.partial(last_kernel, scale),
        shape((ext, own_rows), BF16),
        [],
        flops,
        (queries, keys, top, sums),
    )
    parts = [kept] + [swap(out[k - 1], t=offsets[k]) for k in range(1, blocks)]
    own_pos = (src * n_tgt + tgt) * own_rows + jnp.arange(own_rows, dtype=jnp.int32)
    own = jnp.stack(grid_coords(own_pos), axis=0)
    return call(
        functools.partial(merge_kernel, scale),
        (shape((2, own_rows), F32), shape((own_rows, width), BF16)),
        [],
        4 * ext * own_rows * len(parts),
        (*parts, own),
    )


def solution(mesh):
    in_specs = (P(("src", "tgt"), None), P("tgt", "src"), P())
    out_specs = (P(None, ("src", "tgt")), P(("src", "tgt"), None))
    return jax.shard_map(
        per_device, mesh=mesh, in_specs=in_specs, out_specs=out_specs, check_vma=False
    )
```

```python
import functools
import math

import jax
import jax.numpy as jnp
from jax import lax
from jax.experimental import pallas as pl
from jax.experimental.pallas import tpu as pltpu
from jax.sharding import PartitionSpec as P

W_GRID = 320
STAT_ROWS = 16
CHUNK = 512
F32, BF16 = jnp.float32, jnp.bfloat16


def grid_coords(pos):
    return (
        (pos % W_GRID).astype(F32) / W_GRID,
        (pos // W_GRID).astype(F32) / W_GRID,
    )


def coord_rows(start, count):
    pos = start + lax.broadcasted_iota(jnp.int32, (STAT_ROWS, count), 1)
    row = lax.broadcasted_iota(jnp.int32, (STAT_ROWS, count), 0)
    gx, gy = pos % W_GRID, pos // W_GRID
    rows = jnp.where(row == 0, 1, 0)
    for index, value in enumerate((gx // 16, gx % 16, gy // 16, gy % 16)):
        rows = jnp.where(row == index + 1, value, rows)
    return rows.astype(BF16)


def split3(value):
    high = value.astype(BF16)
    rest = value - high.astype(F32)
    mid = rest.astype(BF16)
    low = (rest - mid.astype(F32)).astype(BF16)
    return [high.astype(F32), mid.astype(F32), low.astype(F32)]


def as_row(column):
    return jnp.transpose(jnp.broadcast_to(column, (column.shape[0], 128)))[0:1, :]


def either(even, odd):
    return jnp.where(lax.axis_index("src") % 2 == 0, even[...], odd[...])


def project(pieces, projt, rows, strip, kext):
    depth, width = pieces[0].shape[0], projt.shape[0]
    src = lax.axis_index("src")
    for step, piece in enumerate(pieces):
        strip[pl.ds(pl.multiple_of((src ^ step) * depth, depth), depth), :] = piece
    kext[0:width, :] = jnp.dot(projt[...], strip[...], preferred_element_type=F32).astype(BF16)
    kext[width:, :] = rows[...]


def attend(queries, kext, scale):
    tops, totals = [], []
    for first in range(0, queries.shape[0], CHUNK):
        part = queries[first : first + CHUNK]
        raw = jnp.dot(part, kext[0 : part.shape[1], :], preferred_element_type=F32)
        top = jnp.max(raw, axis=1, keepdims=True)
        weights = jnp.exp2((raw - top) * scale).astype(BF16)
        tops.append(as_row(top))
        totals.append(
            lax.dot_general(
                kext[...], weights, (((1,), (1,)), ((), ())), preferred_element_type=F32
            )
        )
    return jnp.concatenate(tops, axis=1), jnp.concatenate(totals, axis=1)


def first_kernel(scale, *refs):
    own, near, one, near_one, two, near_two, projt, proj, rows, *refs = refs
    *sources, top_ref, sums_ref, query_ref, kext, strip = refs
    pieces = [own[...], near[...], either(one, near_two), either(two, near_one)]
    project(pieces, projt, rows, strip, kext)
    source = jnp.concatenate([ref[...] for ref in sources], axis=0)
    queries = jnp.dot(source, proj[...], preferred_element_type=F32).astype(BF16)
    query_ref[...] = queries
    top_ref[...], sums_ref[...] = attend(queries, kext, scale)


def emit(first, state, kext, out_refs, scale):
    lanes = out_refs[0].shape[1]
    span = slice(first * lanes, (first + len(out_refs)) * lanes)
    top_ref, sums_ref, query_ref = state
    queries = query_ref[span, :]
    top1, (top2, sums2) = top_ref[:, span], attend(queries, kext, scale)
    top = jnp.maximum(top1, top2)
    sums = sums_ref[:, span] * jnp.exp2((top1 - top) * scale) + sums2 * jnp.exp2(
        (top2 - top) * scale
    )
    width = queries.shape[1]
    stats = sums[width:]
    coord_x = stats[1:2] * 16.0 + stats[2:3]
    coord_y = stats[3:4] * 16.0 + stats[4:5]
    parts = split3(top) + split3(stats[0:1]) + split3(coord_x) + split3(coord_y)
    parts.append(jnp.zeros((STAT_ROWS - len(parts), top.shape[1]), F32))
    out = jnp.concatenate([sums[0:width], *parts], axis=0).astype(BF16)
    for index, out_ref in enumerate(out_refs):
        out_ref[...] = out[:, index * lanes : (index + 1) * lanes]


def second_kernel(first, scale, *refs):
    one, near_one, two, near_two, cross, near_cross, projt, rows, *refs = refs
    state, (*out_refs, kext, strip) = refs[:3], refs[3:]
    pieces = [either(near_two, one), either(near_one, two), cross[...], near_cross[...]]
    project(pieces, projt, rows, strip, kext)
    emit(first, state, kext, out_refs, scale)


def third_kernel(first, scale, *refs):
    state, kext, out_refs = refs[:3], refs[3], refs[4:]
    emit(first, state, kext, out_refs, scale)


def joined(stats, index):
    rows = stats[3 * index : 3 * index + 3]
    return rows[0:1] + rows[1:2] + rows[2:3]


def merged(scale, parts):
    top = functools.reduce(jnp.maximum, [t for t, _ in parts])
    return top, sum(jnp.exp2((t - top) * scale) * sums for t, sums in parts)


def unpacked(ref):
    width = ref.shape[0] - STAT_ROWS
    stats = ref[width:, :].astype(F32)
    rows = [ref[0:width, :].astype(F32), *(joined(stats, k) for k in (1, 2, 3))]
    return joined(stats, 0), jnp.concatenate([*rows, jnp.zeros((5, ref.shape[1]), F32)], axis=0)


def gather_kernel(scale, *refs):
    *parts, top_ref, sums_ref = refs
    top_ref[...], sums_ref[...] = merged(scale, [unpacked(p) for p in parts])


def merge_kernel(scale, *refs):
    *parts, top_ref, sums_ref, own_ref, flow_ref, matched_ref = refs
    _, sums = merged(scale, [(top_ref[...], sums_ref[...]), *(unpacked(p) for p in parts)])
    width = matched_ref.shape[1]
    total = sums[width : width + 1]
    flow_ref[...] = sums[width + 1 : width + 3] / (total * W_GRID) - own_ref[...]
    matched_ref[...] = jnp.transpose(sums[0:width] / total).astype(matched_ref.dtype)


def call(kernel, outs, scratch, flops, args):
    size = lambda a: math.prod(a.shape) * a.dtype.itemsize
    return pl.pallas_call(
        kernel,
        out_shape=outs,
        scratch_shapes=scratch,
        compiler_params=pltpu.CompilerParams(vmem_limit_bytes=32 * 2**20),
        cost_estimate=pl.CostEstimate(
            flops=flops,
            bytes_accessed=sum(map(size, args)) + sum(map(size, jax.tree.leaves(outs))),
            transcendentals=0,
        ),
    )(*args)


def after(value, *others):
    def kernel(value_ref, *refs):
        refs[-1][...] = value_ref[...]

    return pl.pallas_call(
        kernel,
        out_shape=jax.ShapeDtypeStruct(value.shape, value.dtype),
        compiler_params=pltpu.CompilerParams(vmem_limit_bytes=8 * 2**20),
    )(value, *others)


def per_device(source_feat, target_feat, proj):
    width = proj.shape[1]
    own_rows = source_feat.shape[0]
    count = target_feat.shape[0]
    n_src, n_tgt = lax.axis_size("src"), lax.axis_size("tgt")
    src, tgt = lax.axis_index("src"), lax.axis_index("tgt")
    scale = math.log2(math.e) * width ** (-0.5)
    axes = ("src", "tgt")

    def permute(x, move):
        pairs = []
        for a in range(n_src):
            for b in range(n_tgt):
                s, t = move(a)
                pairs.append((a * n_tgt + b, (a ^ s) * n_tgt + (b ^ t)))
        return lax.ppermute(x, axes, pairs)

    def swap(x, s=0, t=0):
        return permute(x, lambda a: (s, t))

    turn_one = lambda a: (2, 0) if a % 2 == 0 else (0, 1)
    turn_two = lambda a: (0, 1) if a % 2 == 0 else (2, 0)
    own = target_feat.T
    near = swap(own, s=1)
    one = permute(own, turn_one)
    two = permute(near, turn_one)
    cross = permute(one, turn_two)
    near_one, near_two = swap(one, s=1), swap(two, s=1)

    blocks = n_tgt // 2
    half = blocks // 2
    offsets = [0, *range(2 * half, n_tgt - 2, 2), n_tgt - 2, *range(2, 2 * half, 2)]
    late = after(source_feat, near)
    sources = [source_feat]
    sources += [swap(source_feat if t == 2 * half else late, t=t) for t in offsets[1:]]

    projt = proj.T
    rows = [coord_rows((tgt ^ k) * count, count) for k in (0, 1)]
    n_q = blocks * own_rows
    ext = width + STAT_ROWS
    shape = jax.ShapeDtypeStruct
    flops = 2 * count * width * (width + 2 * n_q)
    kext = shape((ext, count), BF16)
    strip = pltpu.VMEM((width, count), BF16)
    message = [shape((ext, own_rows), BF16)] * half
    state = call(
        functools.partial(first_kernel, scale),
        (shape((1, n_q), F32), shape((ext, n_q), F32), shape((n_q, width), BF16)),
        [pltpu.VMEM(kext.shape, BF16), strip],
        flops,
        (own, near, one, near_one, two, near_two, projt, proj, rows[0], *sources),
    )
    near_cross = swap(after(cross, state[0]), s=1)
    *sent, keys = call(
        functools.partial(second_kernel, half, scale),
        (*message, kext),
        [strip],
        flops,
        (one, near_one, two, near_two, cross, near_cross, projt, rows[1], *state),
    )
    kept, *rest = call(
        functools.partial(third_kernel, 0, scale), message, [], flops, (*state, keys)
    )
    sent = [swap(x, t=t) for x, t in zip(sent, offsets[half:])]
    rest = [swap(x, t=t) for x, t in zip(rest, offsets[1:half])]
    top, sums = call(
        functools.partial(gather_kernel, scale),
        (shape((1, own_rows), F32), shape((width + 8, own_rows), F32)),
        [],
        2 * 10**9,
        (kept, *sent),
    )
    own_pos = (src * n_tgt + tgt) * own_rows + jnp.arange(own_rows, dtype=jnp.int32)
    own_coords = jnp.stack(grid_coords(own_pos), axis=0)
    return call(
        functools.partial(merge_kernel, scale),
        (shape((2, own_rows), F32), shape((own_rows, width), BF16)),
        [],
        4 * ext * own_rows * half,
        (*rest, top, sums, own_coords),
    )


def solution(mesh):
    in_specs = (P(("src", "tgt"), None), P("tgt", "src"), P())
    out_specs = (P(None, ("src", "tgt")), P(("src", "tgt"), None))
    return jax.shard_map(
        per_device, mesh=mesh, in_specs=in_specs, out_specs=out_specs, check_vma=False
    )
```

```python
import functools
import math

import jax
import jax.numpy as jnp
from jax import lax
from jax.experimental import pallas as pl
from jax.experimental.pallas import tpu as pltpu
from jax.sharding import PartitionSpec as P

W_GRID = 320
STAT_ROWS = 16
CHUNK = 512
F32, BF16 = jnp.float32, jnp.bfloat16


def grid_coords(pos):
    return (
        (pos % W_GRID).astype(F32) / W_GRID,
        (pos // W_GRID).astype(F32) / W_GRID,
    )


def coord_rows(start, count):
    pos = start + lax.broadcasted_iota(jnp.int32, (STAT_ROWS, count), 1)
    row = lax.broadcasted_iota(jnp.int32, (STAT_ROWS, count), 0)
    gx, gy = pos % W_GRID, pos // W_GRID
    rows = jnp.where(row == 0, 1, 0)
    for index, value in enumerate((gx // 16, gx % 16, gy // 16, gy % 16)):
        rows = jnp.where(row == index + 1, value, rows)
    return rows.astype(BF16)


def split3(value):
    high = value.astype(BF16)
    rest = value - high.astype(F32)
    mid = rest.astype(BF16)
    low = (rest - mid.astype(F32)).astype(BF16)
    return [high.astype(F32), mid.astype(F32), low.astype(F32)]


def as_row(column):
    return jnp.transpose(jnp.broadcast_to(column, (column.shape[0], 128)))[0:1, :]


def either(even, odd):
    return jnp.where(lax.axis_index("src") % 2 == 0, even[...], odd[...])


def project(pieces, projt, rows, strip, kext):
    depth, width = pieces[0].shape[0], projt.shape[0]
    src = lax.axis_index("src")
    for step, piece in enumerate(pieces):
        strip[pl.ds(pl.multiple_of((src ^ step) * depth, depth), depth), :] = piece
    kext[0:width, :] = jnp.dot(projt[...], strip[...], preferred_element_type=F32).astype(BF16)
    kext[width:, :] = rows[...]


def attend(queries, kext, scale):
    tops, totals = [], []
    for first in range(0, queries.shape[0], CHUNK):
        part = queries[first : first + CHUNK]
        raw = jnp.dot(part, kext[0 : part.shape[1], :], preferred_element_type=F32)
        top = jnp.max(raw, axis=1, keepdims=True)
        weights = jnp.exp2((raw - top) * scale).astype(BF16)
        tops.append(as_row(top))
        totals.append(
            lax.dot_general(
                kext[...], weights, (((1,), (1,)), ((), ())), preferred_element_type=F32
            )
        )
    return jnp.concatenate(tops, axis=1), jnp.concatenate(totals, axis=1)


def start(sources, proj, kext, state, scale):
    top_ref, sums_ref, query_ref = state
    source = jnp.concatenate([ref[...] for ref in sources], axis=0)
    queries = jnp.dot(source, proj[...], preferred_element_type=F32).astype(BF16)
    query_ref[...] = queries
    top_ref[...], sums_ref[...] = attend(queries, kext, scale)


def first_kernel(early, scale, *refs):
    own, near, one, near_one, two, near_two, projt, proj, rows, *refs = refs
    sources, state, (kext, strip) = refs[:early], refs[-5:-2], refs[-2:]
    pieces = [own[...], near[...], either(one, near_two), either(two, near_one)]
    project(pieces, projt, rows, strip, kext)
    start(sources, proj, kext, state, scale)


def rest_kernel(scale, *refs):
    *sources, proj, kext = refs[:-3]
    start(sources, proj, kext, refs[-3:], scale)


def emit(states, kext, out_refs, scale):
    lanes = out_refs[0].shape[1]
    top1 = jnp.concatenate([top[:, first:end] for (top, _, _), first, end in states], axis=1)
    sums1 = jnp.concatenate([sums[:, first:end] for (_, sums, _), first, end in states], axis=1)
    queries = jnp.concatenate([q[first:end, :] for (_, _, q), first, end in states], axis=0)
    top2, sums2 = attend(queries, kext, scale)
    top = jnp.maximum(top1, top2)
    sums = sums1 * jnp.exp2((top1 - top) * scale) + sums2 * jnp.exp2((top2 - top) * scale)
    width = queries.shape[1]
    stats = sums[width:]
    coord_x = stats[1:2] * 16.0 + stats[2:3]
    coord_y = stats[3:4] * 16.0 + stats[4:5]
    parts = split3(top) + split3(stats[0:1]) + split3(coord_x) + split3(coord_y)
    parts.append(jnp.zeros((STAT_ROWS - len(parts), top.shape[1]), F32))
    out = jnp.concatenate([sums[0:width], *parts], axis=0).astype(BF16)
    for index, out_ref in enumerate(out_refs):
        out_ref[...] = out[:, index * lanes : (index + 1) * lanes]


def second_kernel(scale, *refs):
    one, near_one, two, near_two, cross, near_cross, projt, rows, *refs = refs
    state, (*out_refs, kext, strip) = refs[:3], refs[3:]
    pieces = [either(near_two, one), either(near_one, two), cross[...], near_cross[...]]
    project(pieces, projt, rows, strip, kext)
    n_q = state[2].shape[0]
    emit([(state, n_q - len(out_refs) * out_refs[0].shape[1], n_q)], kext, out_refs, scale)


def third_kernel(scale, *refs):
    state, others, kext, out_refs = refs[:3], refs[3:6], refs[6], refs[7:]
    n_q = state[2].shape[0]
    n_others = len(out_refs) * out_refs[0].shape[1] - n_q
    states = [(state, 0, n_q)] + ([(others, 0, n_others)] if n_others else [])
    emit(states, kext, out_refs, scale)


def joined(stats, index):
    rows = stats[3 * index : 3 * index + 3]
    return rows[0:1] + rows[1:2] + rows[2:3]


def merged(scale, parts):
    top = functools.reduce(jnp.maximum, [t for t, _ in parts])
    return top, sum(jnp.exp2((t - top) * scale) * sums for t, sums in parts)


def unpacked(ref):
    width = ref.shape[0] - STAT_ROWS
    stats = ref[width:, :].astype(F32)
    rows = [ref[0:width, :].astype(F32), *(joined(stats, k) for k in (1, 2, 3))]
    return joined(stats, 0), jnp.concatenate([*rows, jnp.zeros((5, ref.shape[1]), F32)], axis=0)


def gather_kernel(scale, *refs):
    *parts, top_ref, sums_ref = refs
    top_ref[...], sums_ref[...] = merged(scale, [unpacked(p) for p in parts])


def merge_kernel(scale, *refs):
    *parts, top_ref, sums_ref, own_ref, flow_ref, matched_ref = refs
    _, sums = merged(scale, [(top_ref[...], sums_ref[...]), *(unpacked(p) for p in parts)])
    width = matched_ref.shape[1]
    total = sums[width : width + 1]
    flow_ref[...] = sums[width + 1 : width + 3] / (total * W_GRID) - own_ref[...]
    matched_ref[...] = jnp.transpose(sums[0:width] / total).astype(matched_ref.dtype)


def call(kernel, outs, scratch, flops, args):
    size = lambda a: math.prod(a.shape) * a.dtype.itemsize
    return pl.pallas_call(
        kernel,
        out_shape=outs,
        scratch_shapes=scratch,
        compiler_params=pltpu.CompilerParams(vmem_limit_bytes=32 * 2**20),
        cost_estimate=pl.CostEstimate(
            flops=flops,
            bytes_accessed=sum(map(size, args)) + sum(map(size, jax.tree.leaves(outs))),
            transcendentals=0,
        ),
    )(*args)


def after(value, *others):
    def kernel(value_ref, *refs):
        refs[-1][...] = value_ref[...]

    return pl.pallas_call(
        kernel,
        out_shape=jax.ShapeDtypeStruct(value.shape, value.dtype),
        compiler_params=pltpu.CompilerParams(vmem_limit_bytes=8 * 2**20),
    )(value, *others)


def per_device(source_feat, target_feat, proj):
    width = proj.shape[1]
    own_rows = source_feat.shape[0]
    count = target_feat.shape[0]
    n_src, n_tgt = lax.axis_size("src"), lax.axis_size("tgt")
    src, tgt = lax.axis_index("src"), lax.axis_index("tgt")
    scale = math.log2(math.e) * width ** (-0.5)
    axes = ("src", "tgt")

    def permute(x, move):
        pairs = []
        for a in range(n_src):
            for b in range(n_tgt):
                s, t = move(a)
                pairs.append((a * n_tgt + b, (a ^ s) * n_tgt + (b ^ t)))
        return lax.ppermute(x, axes, pairs)

    def swap(x, s=0, t=0):
        return permute(x, lambda a: (s, t))

    turn_one = lambda a: (2, 0) if a % 2 == 0 else (0, 1)
    turn_two = lambda a: (0, 1) if a % 2 == 0 else (2, 0)
    own = target_feat.T
    near = swap(own, s=1)
    one = permute(own, turn_one)
    two = permute(near, turn_one)
    cross = permute(one, turn_two)
    near_one, near_two = swap(one, s=1), swap(two, s=1)

    blocks = n_tgt // 2
    half = blocks // 2
    offsets = [0, *range(2 * half, n_tgt - 2, 2), n_tgt - 2, *range(2, 2 * half, 2)]
    late = after(source_feat, near)
    sources = [source_feat]
    sources += [swap(source_feat if t == 2 * half else late, t=t) for t in offsets[1:]]

    projt = proj.T
    rows = [coord_rows((tgt ^ k) * count, count) for k in (0, 1)]
    n_q = blocks * own_rows
    ext = width + STAT_ROWS
    shape = jax.ShapeDtypeStruct
    flops = 2 * count * width * (width + 2 * n_q)
    kext = shape((ext, count), BF16)
    strip = pltpu.VMEM((width, count), BF16)
    message = [shape((ext, own_rows), BF16)] * half
    state = lambda n_q: (shape((1, n_q), F32), shape((ext, n_q), F32), shape((n_q, width), BF16))
    *first, first_keys = call(
        functools.partial(first_kernel, half, scale),
        (*state(half * own_rows), kext),
        [strip],
        flops,
        (own, near, one, near_one, two, near_two, projt, proj, rows[0], *sources),
    )
    near_cross = swap(after(cross, first[0]), s=1)
    others = call(
        functools.partial(rest_kernel, scale),
        state(n_q - half * own_rows),
        [],
        flops,
        (*sources[half:], proj, first_keys),
    )
    *sent, keys = call(
        functools.partial(second_kernel, scale),
        (*message, kext),
        [strip],
        flops,
        (one, near_one, two, near_two, cross, near_cross, projt, rows[1], *others),
    )
    kept, *rest = call(
        functools.partial(third_kernel, scale), message, [], flops, (*first, *others, keys)
    )
    sent = [swap(x, t=t) for x, t in zip(sent, offsets[half:])]
    rest = [swap(x, t=t) for x, t in zip(rest, offsets[1:half])]
    top, sums = call(
        functools.partial(gather_kernel, scale),
        (shape((1, own_rows), F32), shape((width + 8, own_rows), F32)),
        [],
        2 * 10**9,
        (kept, *sent),
    )
    own_pos = (src * n_tgt + tgt) * own_rows + jnp.arange(own_rows, dtype=jnp.int32)
    own_coords = jnp.stack(grid_coords(own_pos), axis=0)
    return call(
        functools.partial(merge_kernel, scale),
        (shape((2, own_rows), F32), shape((own_rows, width), BF16)),
        [],
        4 * ext * own_rows * half,
        (*rest, top, sums, own_coords),
    )


def solution(mesh):
    in_specs = (P(("src", "tgt"), None), P("tgt", "src"), P())
    out_specs = (P(None, ("src", "tgt")), P(("src", "tgt"), None))
    return jax.shard_map(
        per_device, mesh=mesh, in_specs=in_specs, out_specs=out_specs, check_vma=False
    )
```

```python
import functools
import math

import jax
import jax.numpy as jnp
from jax import lax
from jax.experimental import pallas as pl
from jax.experimental.pallas import tpu as pltpu
from jax.sharding import PartitionSpec as P

W_GRID = 320
STAT_ROWS = 16
CHUNK = 512
F32, BF16 = jnp.float32, jnp.bfloat16


def grid_coords(pos):
    return (
        (pos % W_GRID).astype(F32) / W_GRID,
        (pos // W_GRID).astype(F32) / W_GRID,
    )


def coord_rows(start, count):
    pos = start + lax.broadcasted_iota(jnp.int32, (STAT_ROWS, count), 1)
    row = lax.broadcasted_iota(jnp.int32, (STAT_ROWS, count), 0)
    gx, gy = pos % W_GRID, pos // W_GRID
    rows = jnp.where(row == 0, 1, 0)
    for index, value in enumerate((gx // 16, gx % 16, gy // 16, gy % 16)):
        rows = jnp.where(row == index + 1, value, rows)
    return rows.astype(BF16)


def split3(value):
    high = value.astype(BF16)
    rest = value - high.astype(F32)
    mid = rest.astype(BF16)
    low = (rest - mid.astype(F32)).astype(BF16)
    return [high.astype(F32), mid.astype(F32), low.astype(F32)]


def as_row(column):
    return jnp.transpose(jnp.broadcast_to(column, (column.shape[0], 128)))[0:1, :]


def either(even, odd):
    return jnp.where(lax.axis_index("src") % 2 == 0, even[...], odd[...])


def project(pieces, projt, rows, strip, kext):
    depth, width = pieces[0].shape[0], projt.shape[0]
    src = lax.axis_index("src")
    for step, piece in enumerate(pieces):
        strip[pl.ds(pl.multiple_of((src ^ step) * depth, depth), depth), :] = piece
    kext[0:width, :] = jnp.dot(projt[...], strip[...], preferred_element_type=F32).astype(BF16)
    kext[width:, :] = rows[...]


def attend(queries, kext, scale):
    tops, totals = [], []
    for first in range(0, queries.shape[0], CHUNK):
        part = queries[first : first + CHUNK]
        raw = jnp.dot(part, kext[0 : part.shape[1], :], preferred_element_type=F32)
        top = jnp.max(raw, axis=1, keepdims=True)
        weights = jnp.exp2((raw - top) * scale).astype(BF16)
        tops.append(as_row(top))
        totals.append(
            lax.dot_general(
                kext[...], weights, (((1,), (1,)), ((), ())), preferred_element_type=F32
            )
        )
    return jnp.concatenate(tops, axis=1), jnp.concatenate(totals, axis=1)


def start(sources, proj, kext, state, scale):
    top_ref, sums_ref, query_ref = state
    source = jnp.concatenate([ref[...] for ref in sources], axis=0)
    queries = jnp.dot(source, proj[...], preferred_element_type=F32).astype(BF16)
    query_ref[...] = queries
    top_ref[...], sums_ref[...] = attend(queries, kext, scale)


def first_kernel(early, scale, *refs):
    own, near, one, near_one, two, near_two, projt, proj, rows, *refs = refs
    sources, state, (kext, strip) = refs[:early], refs[-5:-2], refs[-2:]
    pieces = [own[...], near[...], either(one, near_two), either(two, near_one)]
    project(pieces, projt, rows, strip, kext)
    start(sources, proj, kext, state, scale)


def rest_kernel(scale, *refs):
    *sources, proj, kext = refs[:-3]
    start(sources, proj, kext, refs[-3:], scale)


def emit(states, kext, out_refs, scale):
    lanes = out_refs[0].shape[1]
    top1 = jnp.concatenate([top[:, first:end] for (top, _, _), first, end in states], axis=1)
    sums1 = jnp.concatenate([sums[:, first:end] for (_, sums, _), first, end in states], axis=1)
    queries = jnp.concatenate([q[first:end, :] for (_, _, q), first, end in states], axis=0)
    top2, sums2 = attend(queries, kext, scale)
    top = jnp.maximum(top1, top2)
    sums = sums1 * jnp.exp2((top1 - top) * scale) + sums2 * jnp.exp2((top2 - top) * scale)
    width = queries.shape[1]
    stats = sums[width:]
    coord_x = stats[1:2] * 16.0 + stats[2:3]
    coord_y = stats[3:4] * 16.0 + stats[4:5]
    parts = split3(top) + split3(stats[0:1]) + split3(coord_x) + split3(coord_y)
    parts.append(jnp.zeros((STAT_ROWS - len(parts), top.shape[1]), F32))
    out = jnp.concatenate([sums[0:width], *parts], axis=0).astype(BF16)
    for index, out_ref in enumerate(out_refs):
        out_ref[...] = out[:, index * lanes : (index + 1) * lanes]


def second_kernel(scale, *refs):
    one, near_one, two, near_two, cross, near_cross, projt, rows, *refs = refs
    state, (*out_refs, kext, strip) = refs[:3], refs[3:]
    pieces = [either(near_two, one), either(near_one, two), cross[...], near_cross[...]]
    project(pieces, projt, rows, strip, kext)
    n_q = state[2].shape[0]
    emit([(state, n_q - len(out_refs) * out_refs[0].shape[1], n_q)], kext, out_refs, scale)


def third_kernel(scale, *refs):
    state, others, kext, out_refs = refs[:3], refs[3:6], refs[6], refs[7:]
    n_q = state[2].shape[0]
    n_others = len(out_refs) * out_refs[0].shape[1] - n_q
    states = [(state, 0, n_q)] + ([(others, 0, n_others)] if n_others else [])
    emit(states, kext, out_refs, scale)


def joined(stats, index):
    rows = stats[3 * index : 3 * index + 3]
    return rows[0:1] + rows[1:2] + rows[2:3]


def merged(scale, parts):
    top = functools.reduce(jnp.maximum, [t for t, _ in parts])
    return top, sum(jnp.exp2((t - top) * scale) * sums for t, sums in parts)


def unpacked(ref):
    width = ref.shape[0] - STAT_ROWS
    stats = ref[width:, :].astype(F32)
    rows = [ref[0:width, :].astype(F32), *(joined(stats, k) for k in (1, 2, 3))]
    return joined(stats, 0), jnp.concatenate([*rows, jnp.zeros((5, ref.shape[1]), F32)], axis=0)


def gather_kernel(scale, *refs):
    *parts, top_ref, sums_ref = refs
    top_ref[...], sums_ref[...] = merged(scale, [unpacked(p) for p in parts])


def merge_kernel(scale, *refs):
    *parts, top_ref, sums_ref, own_ref, flow_ref, matched_ref = refs
    _, sums = merged(scale, [(top_ref[...], sums_ref[...]), *(unpacked(p) for p in parts)])
    width = matched_ref.shape[1]
    total = sums[width : width + 1]
    flow_ref[...] = sums[width + 1 : width + 3] / (total * W_GRID) - own_ref[...]
    matched_ref[...] = jnp.transpose((sums[0:width] * (1.0 / total)).astype(matched_ref.dtype))


def call(kernel, outs, scratch, flops, args):
    size = lambda a: math.prod(a.shape) * a.dtype.itemsize
    return pl.pallas_call(
        kernel,
        out_shape=outs,
        scratch_shapes=scratch,
        compiler_params=pltpu.CompilerParams(vmem_limit_bytes=32 * 2**20),
        cost_estimate=pl.CostEstimate(
            flops=flops,
            bytes_accessed=sum(map(size, args)) + sum(map(size, jax.tree.leaves(outs))),
            transcendentals=0,
        ),
    )(*args)


def after(value, *others):
    def kernel(value_ref, *refs):
        refs[-1][...] = value_ref[...]

    return pl.pallas_call(
        kernel,
        out_shape=jax.ShapeDtypeStruct(value.shape, value.dtype),
        compiler_params=pltpu.CompilerParams(vmem_limit_bytes=8 * 2**20),
    )(value, *others)


def per_device(source_feat, target_feat, proj):
    width = proj.shape[1]
    own_rows = source_feat.shape[0]
    count = target_feat.shape[0]
    n_src, n_tgt = lax.axis_size("src"), lax.axis_size("tgt")
    src, tgt = lax.axis_index("src"), lax.axis_index("tgt")
    scale = math.log2(math.e) * width ** (-0.5)
    axes = ("src", "tgt")

    def permute(x, move):
        pairs = []
        for a in range(n_src):
            for b in range(n_tgt):
                s, t = move(a)
                pairs.append((a * n_tgt + b, (a ^ s) * n_tgt + (b ^ t)))
        return lax.ppermute(x, axes, pairs)

    def swap(x, s=0, t=0):
        return permute(x, lambda a: (s, t))

    turn_one = lambda a: (2, 0) if a % 2 == 0 else (0, 1)
    turn_two = lambda a: (0, 1) if a % 2 == 0 else (2, 0)
    own = target_feat.T
    near = swap(own, s=1)
    one = permute(own, turn_one)
    two = permute(near, turn_one)
    cross = permute(one, turn_two)
    near_one, near_two = swap(one, s=1), swap(two, s=1)

    blocks = n_tgt // 2
    half = blocks // 2
    offsets = [0, *range(2 * half, n_tgt - 2, 2), n_tgt - 2, *range(2, 2 * half, 2)]
    late = after(source_feat, near)
    sources = [source_feat]
    sources += [swap(source_feat if t == 2 * half else late, t=t) for t in offsets[1:]]

    projt = proj.T
    rows = [coord_rows((tgt ^ k) * count, count) for k in (0, 1)]
    n_q = blocks * own_rows
    ext = width + STAT_ROWS
    shape = jax.ShapeDtypeStruct
    flops = 2 * count * width * (width + 2 * n_q)
    kext = shape((ext, count), BF16)
    strip = pltpu.VMEM((width, count), BF16)
    message = [shape((ext, own_rows), BF16)] * half
    state = lambda n_q: (shape((1, n_q), F32), shape((ext, n_q), F32), shape((n_q, width), BF16))
    *first, first_keys = call(
        functools.partial(first_kernel, half, scale),
        (*state(half * own_rows), kext),
        [strip],
        flops,
        (own, near, one, near_one, two, near_two, projt, proj, rows[0], *sources),
    )
    near_cross = swap(after(cross, first[0]), s=1)
    others = call(
        functools.partial(rest_kernel, scale),
        state(n_q - half * own_rows),
        [],
        flops,
        (*sources[half:], proj, first_keys),
    )
    *sent, keys = call(
        functools.partial(second_kernel, scale),
        (*message, kext),
        [strip],
        flops,
        (one, near_one, two, near_two, cross, near_cross, projt, rows[1], *others),
    )
    kept, *rest = call(
        functools.partial(third_kernel, scale), message, [], flops, (*first, *others, keys)
    )
    sent = [swap(x, t=t) for x, t in zip(sent, offsets[half:])]
    rest = [swap(x, t=t) for x, t in zip(rest, offsets[1:half])]
    top, sums = call(
        functools.partial(gather_kernel, scale),
        (shape((1, own_rows), F32), shape((width + 8, own_rows), F32)),
        [],
        2 * 10**9,
        (kept, *sent),
    )
    own_pos = (src * n_tgt + tgt) * own_rows + jnp.arange(own_rows, dtype=jnp.int32)
    own_coords = jnp.stack(grid_coords(own_pos), axis=0)
    return call(
        functools.partial(merge_kernel, scale),
        (shape((2, own_rows), F32), shape((own_rows, width), BF16)),
        [],
        4 * ext * own_rows * half,
        (*rest, top, sums, own_coords),
    )


def solution(mesh):
    in_specs = (P(("src", "tgt"), None), P("tgt", "src"), P())
    out_specs = (P(None, ("src", "tgt")), P(("src", "tgt"), None))
    return jax.shard_map(
        per_device, mesh=mesh, in_specs=in_specs, out_specs=out_specs, check_vma=False
    )
```

```python
import functools
import math

import jax
import jax.numpy as jnp
from jax import lax
from jax.experimental import pallas as pl
from jax.experimental.pallas import tpu as pltpu
from jax.sharding import PartitionSpec as P

W_GRID = 320
STAT_ROWS = 16
CHUNK = 512
F32, BF16 = jnp.float32, jnp.bfloat16


def grid_coords(pos):
    return (
        (pos % W_GRID).astype(F32) / W_GRID,
        (pos // W_GRID).astype(F32) / W_GRID,
    )


def coord_rows(start, count):
    pos = start + lax.broadcasted_iota(jnp.int32, (STAT_ROWS, count), 1)
    row = lax.broadcasted_iota(jnp.int32, (STAT_ROWS, count), 0)
    gx, gy = pos % W_GRID, pos // W_GRID
    rows = jnp.where(row == 0, 1, 0)
    for index, value in enumerate((gx // 16, gx % 16, gy // 16, gy % 16)):
        rows = jnp.where(row == index + 1, value, rows)
    return rows.astype(BF16)


def split3(value):
    high = value.astype(BF16)
    rest = value - high.astype(F32)
    mid = rest.astype(BF16)
    low = (rest - mid.astype(F32)).astype(BF16)
    return [high.astype(F32), mid.astype(F32), low.astype(F32)]


def as_row(column):
    return jnp.transpose(jnp.broadcast_to(column, (column.shape[0], 128)))[0:1, :]


def either(even, odd):
    return jnp.where(lax.axis_index("src") % 2 == 0, even[...], odd[...])


def project(pieces, projt, rows, strip, kext):
    depth, width = pieces[0].shape[0], projt.shape[0]
    src = lax.axis_index("src")
    for step, piece in enumerate(pieces):
        strip[pl.ds(pl.multiple_of((src ^ step) * depth, depth), depth), :] = piece
    kext[0:width, :] = jnp.dot(projt[...], strip[...], preferred_element_type=F32).astype(BF16)
    kext[width:, :] = rows[...]


def attend(queries, kext, scale):
    tops, totals = [], []
    for first in range(0, queries.shape[0], CHUNK):
        part = queries[first : first + CHUNK]
        raw = jnp.dot(part, kext[0 : part.shape[1], :], preferred_element_type=F32)
        top = jnp.max(raw, axis=1, keepdims=True)
        weights = jnp.exp2((raw - top) * scale).astype(BF16)
        tops.append(as_row(top))
        totals.append(
            lax.dot_general(
                kext[...], weights, (((1,), (1,)), ((), ())), preferred_element_type=F32
            )
        )
    return jnp.concatenate(tops, axis=1), jnp.concatenate(totals, axis=1)


def start(sources, proj, kext, state, scale):
    top_ref, sums_ref, query_ref = state
    source = jnp.concatenate([ref[...] for ref in sources], axis=0)
    queries = jnp.dot(source, proj[...], preferred_element_type=F32).astype(BF16)
    query_ref[...] = queries
    top_ref[...], sums_ref[...] = attend(queries, kext, scale)


def first_kernel(early, scale, *refs):
    own, near, one, near_one, two, near_two, projt, proj, rows, *refs = refs
    sources, state, (kext, strip) = refs[:early], refs[-5:-2], refs[-2:]
    pieces = [own[...], near[...], either(one, near_two), either(two, near_one)]
    project(pieces, projt, rows, strip, kext)
    start(sources, proj, kext, state, scale)


def rest_kernel(scale, *refs):
    *sources, proj, kext = refs[:-3]
    start(sources, proj, kext, refs[-3:], scale)


def emit(states, kext, out_refs, scale):
    lanes = out_refs[0].shape[1]
    top1 = jnp.concatenate([top[:, first:end] for (top, _, _), first, end in states], axis=1)
    sums1 = jnp.concatenate([sums[:, first:end] for (_, sums, _), first, end in states], axis=1)
    queries = jnp.concatenate([q[first:end, :] for (_, _, q), first, end in states], axis=0)
    top2, sums2 = attend(queries, kext, scale)
    top = jnp.maximum(top1, top2)
    sums = sums1 * jnp.exp2((top1 - top) * scale) + sums2 * jnp.exp2((top2 - top) * scale)
    width = queries.shape[1]
    stats = sums[width:]
    coord_x = stats[1:2] * 16.0 + stats[2:3]
    coord_y = stats[3:4] * 16.0 + stats[4:5]
    parts = split3(top) + split3(stats[0:1]) + split3(coord_x) + split3(coord_y)
    parts.append(jnp.zeros((STAT_ROWS - len(parts), top.shape[1]), F32))
    out = jnp.concatenate([sums[0:width], *parts], axis=0).astype(BF16)
    for index, out_ref in enumerate(out_refs):
        out_ref[...] = out[:, index * lanes : (index + 1) * lanes]


def second_kernel(scale, *refs):
    one, near_one, two, near_two, cross, near_cross, projt, rows, *refs = refs
    state, (*out_refs, kext, strip) = refs[:3], refs[3:]
    pieces = [either(near_two, one), either(near_one, two), cross[...], near_cross[...]]
    project(pieces, projt, rows, strip, kext)
    n_q = state[2].shape[0]
    emit([(state, n_q - len(out_refs) * out_refs[0].shape[1], n_q)], kext, out_refs, scale)


def third_kernel(scale, *refs):
    state, others, kext, out_refs = refs[:3], refs[3:6], refs[6], refs[7:]
    n_q = state[2].shape[0]
    n_others = len(out_refs) * out_refs[0].shape[1] - n_q
    states = [(state, 0, n_q)] + ([(others, 0, n_others)] if n_others else [])
    emit(states, kext, out_refs, scale)


def joined(stats, index):
    rows = stats[3 * index : 3 * index + 3]
    return rows[0:1] + rows[1:2] + rows[2:3]


def merged(scale, parts):
    top = functools.reduce(jnp.maximum, [t for t, _ in parts])
    return top, sum(jnp.exp2((t - top) * scale) * sums for t, sums in parts)


def unpacked(ref):
    width = ref.shape[0] - STAT_ROWS
    stats = ref[width:, :].astype(F32)
    rows = [ref[0:width, :].astype(F32), *(joined(stats, k) for k in (1, 2, 3))]
    return joined(stats, 0), jnp.concatenate([*rows, jnp.zeros((5, ref.shape[1]), F32)], axis=0)


def gather_kernel(scale, *refs):
    *parts, top_ref, sums_ref = refs
    top_ref[...], sums_ref[...] = merged(scale, [unpacked(p) for p in parts])


def merge_kernel(scale, *refs):
    *parts, top_ref, sums_ref, own_ref, flow_ref, matched_ref = refs
    _, sums = merged(scale, [(top_ref[...], sums_ref[...]), *(unpacked(p) for p in parts)])
    width = matched_ref.shape[1]
    total = sums[width : width + 1]
    flow_ref[...] = sums[width + 1 : width + 3] / (total * W_GRID) - own_ref[...]
    matched_ref[...] = jnp.transpose(sums[0:width] / total).astype(matched_ref.dtype)


def call(kernel, outs, scratch, flops, args):
    size = lambda a: math.prod(a.shape) * a.dtype.itemsize
    return pl.pallas_call(
        kernel,
        out_shape=outs,
        scratch_shapes=scratch,
        compiler_params=pltpu.CompilerParams(vmem_limit_bytes=32 * 2**20),
        cost_estimate=pl.CostEstimate(
            flops=flops,
            bytes_accessed=sum(map(size, args)) + sum(map(size, jax.tree.leaves(outs))),
            transcendentals=0,
        ),
    )(*args)


def after(value, *others):
    def kernel(value_ref, *refs):
        refs[-1][...] = value_ref[...]

    return pl.pallas_call(
        kernel,
        out_shape=jax.ShapeDtypeStruct(value.shape, value.dtype),
        compiler_params=pltpu.CompilerParams(vmem_limit_bytes=8 * 2**20),
    )(value, *others)


def per_device(source_feat, target_feat, proj):
    width = proj.shape[1]
    own_rows = source_feat.shape[0]
    count = target_feat.shape[0]
    n_src, n_tgt = lax.axis_size("src"), lax.axis_size("tgt")
    src, tgt = lax.axis_index("src"), lax.axis_index("tgt")
    scale = math.log2(math.e) * width ** (-0.5)
    axes = ("src", "tgt")

    def permute(x, move):
        pairs = []
        for a in range(n_src):
            for b in range(n_tgt):
                s, t = move(a)
                pairs.append((a * n_tgt + b, (a ^ s) * n_tgt + (b ^ t)))
        return lax.ppermute(x, axes, pairs)

    def swap(x, s=0, t=0):
        return permute(x, lambda a: (s, t))

    turn_one = lambda a: (2, 0) if a % 2 == 0 else (0, 1)
    turn_two = lambda a: (0, 1) if a % 2 == 0 else (2, 0)
    own = target_feat.T
    near = swap(own, s=1)
    one = permute(own, turn_one)
    two = permute(near, turn_one)
    cross = permute(one, turn_two)
    near_one, near_two = swap(one, s=1), swap(two, s=1)

    blocks = n_tgt // 2
    half = blocks // 2
    offsets = list(range(0, n_tgt, 2))
    late = after(source_feat, near)
    sources = [source_feat]
    sources += [swap(source_feat if t == offsets[-1] else late, t=t) for t in offsets[1:]]

    projt = proj.T
    rows = [coord_rows((tgt ^ k) * count, count) for k in (0, 1)]
    n_q = blocks * own_rows
    ext = width + STAT_ROWS
    shape = jax.ShapeDtypeStruct
    flops = 2 * count * width * (width + 2 * n_q)
    kext = shape((ext, count), BF16)
    strip = pltpu.VMEM((width, count), BF16)
    message = [shape((ext, own_rows), BF16)] * half
    state = lambda n_q: (shape((1, n_q), F32), shape((ext, n_q), F32), shape((n_q, width), BF16))
    *first, first_keys = call(
        functools.partial(first_kernel, half, scale),
        (*state(half * own_rows), kext),
        [strip],
        flops,
        (own, near, one, near_one, two, near_two, projt, proj, rows[0], *sources),
    )
    near_cross = swap(after(cross, first[0]), s=1)
    others = call(
        functools.partial(rest_kernel, scale),
        state(n_q - half * own_rows),
        [],
        flops,
        (*sources[half:], proj, first_keys),
    )
    *sent, keys = call(
        functools.partial(second_kernel, scale),
        (*message, kext),
        [strip],
        flops,
        (one, near_one, two, near_two, cross, near_cross, projt, rows[1], *others),
    )
    kept, *rest = call(
        functools.partial(third_kernel, scale), message, [], flops, (*first, *others, keys)
    )
    sent = [swap(x, t=t) for x, t in zip(sent, offsets[half:])]
    rest = [swap(x, t=t) for x, t in zip(rest, offsets[1:half])]
    top, sums = call(
        functools.partial(gather_kernel, scale),
        (shape((1, own_rows), F32), shape((width + 8, own_rows), F32)),
        [],
        2 * 10**9,
        (kept, *sent),
    )
    own_pos = (src * n_tgt + tgt) * own_rows + jnp.arange(own_rows, dtype=jnp.int32)
    own_coords = jnp.stack(grid_coords(own_pos), axis=0)
    return call(
        functools.partial(merge_kernel, scale),
        (shape((2, own_rows), F32), shape((own_rows, width), BF16)),
        [],
        4 * ext * own_rows * half,
        (*rest, top, sums, own_coords),
    )


def solution(mesh):
    in_specs = (P(("src", "tgt"), None), P("tgt", "src"), P())
    out_specs = (P(None, ("src", "tgt")), P(("src", "tgt"), None))
    return jax.shard_map(
        per_device, mesh=mesh, in_specs=in_specs, out_specs=out_specs, check_vma=False
    )
```

```python
import functools
import math

import jax
import jax.numpy as jnp
from jax import lax
from jax.experimental import pallas as pl
from jax.experimental.pallas import tpu as pltpu
from jax.sharding import PartitionSpec as P

W_GRID = 320
STAT_ROWS = 16
CHUNK = 512
F32, BF16 = jnp.float32, jnp.bfloat16


def grid_coords(pos):
    return (
        (pos % W_GRID).astype(F32) / W_GRID,
        (pos // W_GRID).astype(F32) / W_GRID,
    )


def coord_rows(start, count):
    pos = start + lax.broadcasted_iota(jnp.int32, (STAT_ROWS, count), 1)
    row = lax.broadcasted_iota(jnp.int32, (STAT_ROWS, count), 0)
    gx, gy = pos % W_GRID, pos // W_GRID
    rows = jnp.where(row == 0, 1, 0)
    for index, value in enumerate((gx // 16, gx % 16, gy // 16, gy % 16)):
        rows = jnp.where(row == index + 1, value, rows)
    return rows.astype(BF16)


def split3(value):
    high = value.astype(BF16)
    rest = value - high.astype(F32)
    mid = rest.astype(BF16)
    low = (rest - mid.astype(F32)).astype(BF16)
    return [high.astype(F32), mid.astype(F32), low.astype(F32)]


def as_row(column):
    return jnp.transpose(jnp.broadcast_to(column, (column.shape[0], 128)))[0:1, :]


def either(odd_first, other):
    return jnp.where(lax.axis_index("src") % 2 == 1, odd_first[...], other[...])


def project(pieces, projt, rows, strip, kext):
    depth, width = pieces[0].shape[0], projt.shape[0]
    src = lax.axis_index("src")
    for step, piece in enumerate(pieces):
        strip[pl.ds(pl.multiple_of((src ^ step) * depth, depth), depth), :] = piece
    kext[0:width, :] = jnp.dot(projt[...], strip[...], preferred_element_type=F32).astype(BF16)
    kext[width:, :] = rows[...]


def attend(queries, kext, scale):
    tops, totals = [], []
    for first in range(0, queries.shape[0], CHUNK):
        part = queries[first : first + CHUNK]
        raw = jnp.dot(part, kext[0 : part.shape[1], :], preferred_element_type=F32)
        top = jnp.max(raw, axis=1, keepdims=True)
        weights = jnp.exp2((raw - top) * scale).astype(BF16)
        tops.append(as_row(top))
        totals.append(
            lax.dot_general(
                kext[...], weights, (((1,), (1,)), ((), ())), preferred_element_type=F32
            )
        )
    return jnp.concatenate(tops, axis=1), jnp.concatenate(totals, axis=1)


def start(sources, proj, kext, state, scale):
    top_ref, sums_ref, query_ref = state
    source = jnp.concatenate([ref[...] for ref in sources], axis=0)
    queries = jnp.dot(source, proj[...], preferred_element_type=F32).astype(BF16)
    query_ref[...] = queries
    top_ref[...], sums_ref[...] = attend(queries, kext, scale)


def first_kernel(early, scale, *refs):
    own, near, one, near_one, two, near_two, projt, proj, rows, *refs = refs
    sources, state, (kext, strip) = refs[:early], refs[-5:-2], refs[-2:]
    pieces = [own[...], near[...], either(one, near_two), either(two, near_one)]
    project(pieces, projt, rows, strip, kext)
    start(sources, proj, kext, state, scale)


def rest_kernel(scale, *refs):
    *sources, proj, kext = refs[:-3]
    start(sources, proj, kext, refs[-3:], scale)


def emit(states, kext, out_refs, scale):
    lanes = out_refs[0].shape[1]
    top1 = jnp.concatenate([top[:, first:end] for (top, _, _), first, end in states], axis=1)
    sums1 = jnp.concatenate([sums[:, first:end] for (_, sums, _), first, end in states], axis=1)
    queries = jnp.concatenate([q[first:end, :] for (_, _, q), first, end in states], axis=0)
    top2, sums2 = attend(queries, kext, scale)
    top = jnp.maximum(top1, top2)
    sums = sums1 * jnp.exp2((top1 - top) * scale) + sums2 * jnp.exp2((top2 - top) * scale)
    width = queries.shape[1]
    stats = sums[width:]
    coord_x = stats[1:2] * 16.0 + stats[2:3]
    coord_y = stats[3:4] * 16.0 + stats[4:5]
    parts = split3(top) + split3(stats[0:1]) + split3(coord_x) + split3(coord_y)
    parts.append(jnp.zeros((STAT_ROWS - len(parts), top.shape[1]), F32))
    out = jnp.concatenate([sums[0:width], *parts], axis=0).astype(BF16)
    for index, out_ref in enumerate(out_refs):
        out_ref[...] = out[:, index * lanes : (index + 1) * lanes]


def second_kernel(scale, *refs):
    one, near_one, two, near_two, cross, near_cross, projt, rows, *refs = refs
    state, (*out_refs, kext, strip) = refs[:3], refs[3:]
    pieces = [either(near_two, one), either(near_one, two), cross[...], near_cross[...]]
    project(pieces, projt, rows, strip, kext)
    n_q = state[2].shape[0]
    emit([(state, n_q - len(out_refs) * out_refs[0].shape[1], n_q)], kext, out_refs, scale)


def third_kernel(scale, *refs):
    state, others, kext, out_refs = refs[:3], refs[3:6], refs[6], refs[7:]
    n_q = state[2].shape[0]
    n_others = len(out_refs) * out_refs[0].shape[1] - n_q
    states = [(state, 0, n_q)] + ([(others, 0, n_others)] if n_others else [])
    emit(states, kext, out_refs, scale)


def joined(stats, index):
    rows = stats[3 * index : 3 * index + 3]
    return rows[0:1] + rows[1:2] + rows[2:3]


def merged(scale, parts):
    top = functools.reduce(jnp.maximum, [t for t, _ in parts])
    return top, sum(jnp.exp2((t - top) * scale) * sums for t, sums in parts)


def unpacked(ref):
    width = ref.shape[0] - STAT_ROWS
    stats = ref[width:, :].astype(F32)
    rows = [ref[0:width, :].astype(F32), *(joined(stats, k) for k in (1, 2, 3))]
    return joined(stats, 0), jnp.concatenate([*rows, jnp.zeros((5, ref.shape[1]), F32)], axis=0)


def gather_kernel(scale, *refs):
    *parts, top_ref, sums_ref = refs
    top_ref[...], sums_ref[...] = merged(scale, [unpacked(p) for p in parts])


def merge_kernel(scale, *refs):
    *parts, top_ref, sums_ref, own_ref, flow_ref, matched_ref = refs
    _, sums = merged(scale, [(top_ref[...], sums_ref[...]), *(unpacked(p) for p in parts)])
    width = matched_ref.shape[1]
    total = sums[width : width + 1]
    flow_ref[...] = sums[width + 1 : width + 3] / (total * W_GRID) - own_ref[...]
    matched_ref[...] = jnp.transpose(sums[0:width] / total).astype(matched_ref.dtype)


def call(kernel, outs, scratch, flops, args):
    size = lambda a: math.prod(a.shape) * a.dtype.itemsize
    return pl.pallas_call(
        kernel,
        out_shape=outs,
        scratch_shapes=scratch,
        compiler_params=pltpu.CompilerParams(vmem_limit_bytes=32 * 2**20),
        cost_estimate=pl.CostEstimate(
            flops=flops,
            bytes_accessed=sum(map(size, args)) + sum(map(size, jax.tree.leaves(outs))),
            transcendentals=0,
        ),
    )(*args)


def after(value, *others):
    def kernel(value_ref, *refs):
        refs[-1][...] = value_ref[...]

    return pl.pallas_call(
        kernel,
        out_shape=jax.ShapeDtypeStruct(value.shape, value.dtype),
        compiler_params=pltpu.CompilerParams(vmem_limit_bytes=8 * 2**20),
    )(value, *others)


def per_device(source_feat, target_feat, proj):
    width = proj.shape[1]
    own_rows = source_feat.shape[0]
    count = target_feat.shape[0]
    n_src, n_tgt = lax.axis_size("src"), lax.axis_size("tgt")
    src, tgt = lax.axis_index("src"), lax.axis_index("tgt")
    scale = math.log2(math.e) * width ** (-0.5)
    axes = ("src", "tgt")

    def permute(x, move):
        pairs = []
        for a in range(n_src):
            for b in range(n_tgt):
                s, t = move(a)
                pairs.append((a * n_tgt + b, (a ^ s) * n_tgt + (b ^ t)))
        return lax.ppermute(x, axes, pairs)

    def swap(x, s=0, t=0):
        return permute(x, lambda a: (s, t))

    turn_one = lambda a: (0, 1) if a % 2 == 0 else (2, 0)
    turn_two = lambda a: (2, 0) if a % 2 == 0 else (0, 1)
    own = target_feat.T
    near = swap(own, s=1)
    one = permute(own, turn_one)
    two = permute(near, turn_one)
    cross = permute(one, turn_two)
    near_one, near_two = swap(one, s=1), swap(two, s=1)

    blocks = n_tgt // 2
    half = blocks // 2
    offsets = [0, *range(2 * half, n_tgt - 2, 2), n_tgt - 2, *range(2, 2 * half, 2)]
    late = after(source_feat, near)
    sources = [source_feat]
    sources += [swap(source_feat if t == 2 * half else late, t=t) for t in offsets[1:]]

    projt = proj.T
    rows = [coord_rows((tgt ^ k) * count, count) for k in (0, 1)]
    n_q = blocks * own_rows
    ext = width + STAT_ROWS
    shape = jax.ShapeDtypeStruct
    flops = 2 * count * width * (width + 2 * n_q)
    kext = shape((ext, count), BF16)
    strip = pltpu.VMEM((width, count), BF16)
    message = [shape((ext, own_rows), BF16)] * half
    state = lambda n_q: (shape((1, n_q), F32), shape((ext, n_q), F32), shape((n_q, width), BF16))
    *first, first_keys = call(
        functools.partial(first_kernel, half, scale),
        (*state(half * own_rows), kext),
        [strip],
        flops,
        (own, near, one, near_one, two, near_two, projt, proj, rows[0], *sources),
    )
    near_cross = swap(after(cross, first[0]), s=1)
    others = call(
        functools.partial(rest_kernel, scale),
        state(n_q - half * own_rows),
        [],
        flops,
        (*sources[half:], proj, first_keys),
    )
    *sent, keys = call(
        functools.partial(second_kernel, scale),
        (*message, kext),
        [strip],
        flops,
        (one, near_one, two, near_two, cross, near_cross, projt, rows[1], *others),
    )
    kept, *rest = call(
        functools.partial(third_kernel, scale), message, [], flops, (*first, *others, keys)
    )
    sent = [swap(x, t=t) for x, t in zip(sent, offsets[half:])]
    rest = [swap(x, t=t) for x, t in zip(rest, offsets[1:half])]
    top, sums = call(
        functools.partial(gather_kernel, scale),
        (shape((1, own_rows), F32), shape((width + 8, own_rows), F32)),
        [],
        2 * 10**9,
        (kept, *sent),
    )
    own_pos = (src * n_tgt + tgt) * own_rows + jnp.arange(own_rows, dtype=jnp.int32)
    own_coords = jnp.stack(grid_coords(own_pos), axis=0)
    return call(
        functools.partial(merge_kernel, scale),
        (shape((2, own_rows), F32), shape((own_rows, width), BF16)),
        [],
        4 * ext * own_rows * half,
        (*rest, top, sums, own_coords),
    )


def solution(mesh):
    in_specs = (P(("src", "tgt"), None), P("tgt", "src"), P())
    out_specs = (P(None, ("src", "tgt")), P(("src", "tgt"), None))
    return jax.shard_map(
        per_device, mesh=mesh, in_specs=in_specs, out_specs=out_specs, check_vma=False
    )
```
